32 devices in a mesh: grp: 2 (over y), bus: 4 (over z), line: 2 (over x), scen: 2 (over core).
Axes of the slice: x: 2, y: 2, z: 4, core: 2. Of those that a mesh axis runs over, the one named last changes fastest.
Arguments:
- injections: float32 [128, 4, 4096], P(('grp', 'bus', 'scen'), None, 'line'), parts along dimension 0, may hold values from -6 to 6
- shift_factors: float32 [8192, 16384], P('line', 'bus'), may hold values from -0.046875 to 0.046875
- line_limits: int32 [8192], P('line'), may hold values from 20 to 149
- overload_cost: float32 [8192], P('line'), may hold values from 0.5 to 5
Outputs:
- line_flows: float32 [128, 8192], P(('grp', 'bus', 'scen'), 'line'), parts along dimension 0
- penalty_gradient: float32 [128, 4, 4096], P(('grp', 'bus', 'scen'), None, 'line'), parts along dimension 0
The draws below stay inside these ranges and needn't reach their ends.
There are 2 independent parts, one for each index of `grp`. The reference program is written for one: setup_inputs(seed, part) draws one part's arguments, and reference() takes and returns one part's arrays. A program takes and returns all parts, laid end to end along the dimension named above; an argument that names none is the same for every part. Nothing has to cross between parts.
Inputs may be any that keep to these rules, and one draw needn't show every extreme that they name: `line_limits`: thermal limits in MW on a 100 MW base.
All inputs are finite; a program needn't handle non-finite values.
Results may differ from the reference program's by a relative error of at most 0.00011.
Values sent between devices are 32-bit elements; how exact they have to be, the bound alone decides.
A program may use at most 128 MiB of HBM per device.

```python
import math
import jax
import jax.numpy as jnp
from jax import lax

B = 16384
L = 8192
S = 64
BSHARD = 4096
N_BUS = 4


def set_ends(array, key, smallest, high):
    extent = array.shape
    spot = [jax.random.randint(jax.random.fold_in(key, axis), (), 0, extent[axis]) for axis in range(len(extent))]
    array = array.at[tuple(spot)].set(smallest)
    longest = extent.index(max(extent))
    spot[longest] = (spot[longest] + 1) % extent[longest]
    return array.at[tuple(spot)].set(high)


def block_scale(key, shape, shards, smallest, high):
    loudness, own = 1.0, jax.random.fold_in(key, 6)
    for axis_at, blocks in shards:
        draws = jnp.exp(jax.random.uniform(jax.random.fold_in(own, axis_at), (blocks,), jnp.float32, smallest / len(shards), high / len(shards)))
        loudness = loudness * jnp.repeat(draws, shape[axis_at] // blocks).reshape([-1 if axis == axis_at else 1 for axis in range(len(shape))])
    return loudness


def normal_values(own_key, dims, spread, most, cuts=(), held_as=jnp.bfloat16):
    values = jax.random.normal(own_key, dims, jnp.float32) * spread
    if len(cuts) > 0:
        values = block_scale(own_key, dims, cuts, -0.22, 0.18) * values
    return jnp.clip(values, min=-most, max=most).astype(held_as)


def setup_inputs(seed: int = 0, part: int = 0) -> dict:
    key_list = jax.random.split(jax.random.key(seed), 5)
    part_splits = jax.random.split(jax.random.fold_in(key_list[4], part), 5)
    return {
        "injections": normal_values(part_splits[0], (S, N_BUS, BSHARD), 1.0, 6.0, ((0, 8), (2, 2)), jnp.float32),
        "shift_factors": normal_values(key_list[1], (L, B), B ** -0.5, 0.046875, ((0, 2), (1, 4)), jnp.float32),
        "line_limits": set_ends(jax.random.randint(key_list[2], (L,), 20, 150), jax.random.fold_in(key_list[2], 1), 20, 149).astype(jnp.int32),
        "overload_cost": jnp.clip(jnp.exp(math.log(5.0) - 2.3025851 * jax.random.uniform(key_list[3], (L,), jnp.float32) ** block_scale(key_list[3], (L,), ((0, 2),), -0.2, 0.2)), 0.5, 5.0),
    }


def reference(injections, shift_factors, line_limits, overload_cost):
    rows = injections.reshape(S, B)
    line_flows = jnp.dot(rows, shift_factors.T, precision=lax.Precision.HIGHEST, preferred_element_type=jnp.float32)
    limits = line_limits.astype(jnp.float32) / 100.0
    excess = jax.nn.relu(line_flows - limits) - jax.nn.relu(-line_flows - limits)
    slopes = 2.0 * overload_cost * excess
    gradient = jnp.dot(slopes, shift_factors, precision=lax.Precision.HIGHEST, preferred_element_type=jnp.float32)
    return line_flows, gradient.reshape(S, N_BUS, BSHARD)
```

```python
import functools

import jax
import jax.numpy as jnp
from jax import lax
from jax.experimental import pallas as pl
from jax.experimental.pallas import tpu as pltpu
from jax.sharding import PartitionSpec as P

MESH = pl.DeviceIdType.MESH
F32 = jnp.float32
BF16 = jnp.bfloat16


def split(value):
    high = value.astype(BF16)
    return high, (value - high.astype(F32)).astype(BF16)


def dot_nt(a, b):
    return lax.dot_general(a, b, (((1,), (1,)), ((), ())), preferred_element_type=F32)


def dot_nn(a, b):
    return jnp.dot(a, b, preferred_element_type=F32)


def kernel(
    dims, inj, lim, cost, fac, flow_out, grad_out,
    snd, xbuf, xs, stage, fhi, flo, p, s_right, s_left, r_left, r_right,
    tot, ss, fsend, frecv, g, gc, hs, hx, own, gout,
    ld_sem, z_send, x_send, c_send, b_recv, right_send, left_send, left_recv, right_recv,
    f_send, f_recv, gc_send, gc_recv, hx_send, hx_recv, go_send, go_recv,
):
    nb, nl, ns, r, bx, lc, w, ch, nbuf, tw = dims
    z, x, c = lax.axis_index("bus"), lax.axis_index("line"), lax.axis_index("scen")
    kc, nch, nt = lc // w, lc // ch, bx // tw
    own_rows = nb * r
    rows = ns * own_rows

    def remote(src, dst, send, recv, where):
        return pltpu.make_async_remote_copy(
            src_ref=src, dst_ref=dst, send_sem=send, recv_sem=recv,
            device_id=where, device_id_type=MESH,
        )

    def load(i):
        start = pl.multiple_of(c * lc + i * ch, ch)
        slot = lax.rem(i, nbuf)
        return pltpu.make_async_copy(fac.at[pl.ds(start, ch), :], stage.at[slot], ld_sem.at[slot])

    for i in range(min(nbuf, nch)):
        load(jnp.int32(i)).start()

    barrier = pltpu.get_barrier_semaphore()
    for axis, here, count in (("bus", z, nb), ("line", x, nl), ("scen", c, ns)):
        for d in range(1, count):
            pl.semaphore_signal(
                barrier, inc=1, device_id={axis: lax.rem(here + d, count)}, device_id_type=MESH
            )

    for k in range(nb):
        snd[k] = inj[:, k, :]
    g[...] = jnp.zeros_like(g)
    pl.semaphore_wait(barrier, nb + nl + ns - 3)

    def block(xh, zz, cc):
        return xbuf.at[xh, pl.ds(pl.multiple_of((cc * nb + zz) * r, r), r), :]

    def over_bus(d):
        to = lax.rem(z + d, nb)
        return remote(snd.at[to], block(x, z, c), z_send.at[d], b_recv.at[x, z, c], {"bus": to})

    def over_line(dx, d):
        zz = lax.rem(z + nb - d, nb)
        return remote(
            block(x, zz, c), block(x, zz, c), x_send.at[dx, d], b_recv.at[x, zz, c],
            {"line": lax.rem(x + dx, nl)},
        )

    def over_core(dx, d, dc):
        zz, xh = lax.rem(z + nb - d, nb), lax.rem(x + nl - dx, nl)
        return remote(
            block(xh, zz, c), block(xh, zz, c), c_send.at[dx, d, dc], b_recv.at[xh, zz, c],
            {"scen": lax.rem(c + dc, ns)},
        )

    def arrived(xh, zz, cc):
        remote(
            block(xh, zz, cc), block(xh, zz, cc), z_send.at[0], b_recv.at[xh, zz, cc],
            {"bus": lax.rem(z + 1, nb)},
        ).wait_recv()

    for d in range(1, nb):
        over_bus(d).start()
    start_row = pl.multiple_of((c * nb + z) * r, r)
    xbuf[x, pl.ds(start_row, r), :] = snd[z]

    def forward(d):
        for dx in range(1, nl):
            over_line(dx, d).start()
        for dc in range(1, ns):
            over_core(0, d, dc).start()

    forward(0)

    def convert(i, carry):
        load(i).wait()
        slot = lax.rem(i, nbuf)
        high, low = split(stage[slot])
        at = pl.ds(pl.multiple_of(i * ch, ch), ch)
        fhi[at, :] = high
        flo[at, :] = low

        @pl.when(i + nbuf < nch)
        def _():
            load(i + nbuf).start()

        return carry

    for n in range(1, nb + 1):
        lax.fori_loop((n - 1) * nch // nb, n * nch // nb, convert, 0)
        if n < nb:
            arrived(x, lax.rem(z + nb - n, nb), c)
            forward(n)
        for dx in range(1, nl):
            xh, zz = lax.rem(x + nl - dx, nl), lax.rem(z + nb - n + 1, nb)
            arrived(xh, zz, c)
            for dc in range(1, ns):
                over_core(dx, n - 1, dc).start()

    for dc in range(1, ns):
        for dx in range(nl):
            for d in range(nb):
                arrived(lax.rem(x + nl - dx, nl), lax.rem(z + nb - d, nb), lax.rem(c + dc, ns))

    for xh in range(nl):
        high, low = split(xbuf[xh])
        xs[:rows, xh * bx:(xh + 1) * bx] = high
        xs[rows:, xh * bx:(xh + 1) * bx] = low

    def to_right(src, k):
        return remote(
            src.at[k], r_left.at[k], right_send.at[k], left_recv.at[k],
            {"bus": lax.rem(z + 1, nb)},
        )

    def to_left(src, k):
        return remote(
            src.at[k], r_right.at[k], left_send.at[k], right_recv.at[k],
            {"bus": lax.rem(z + nb - 1, nb)},
        )

    lag_left = jnp.minimum(2 * z, kc - 1)
    lag_right = jnp.minimum(2 * (nb - 1 - z), kc - 1)

    def relay(s):
        k = s - lag_left

        @pl.when((z > 0) & (k >= 0) & (k < kc))
        def _():
            to_right(s_right, k).wait_recv()

            @pl.when(z < nb - 1)
            def _():
                s_right[k] = r_left[k] + p[k]
                to_right(s_right, k).start()

        m = s - lag_right

        @pl.when((z < nb - 1) & (m >= 0) & (m < kc))
        def _():
            to_left(s_left, m).wait_recv()

            @pl.when(z > 0)
            def _():
                s_left[m] = r_right[m] + p[m]
                to_left(s_left, m).start()

    def lines_of(k):
        return pl.ds(pl.multiple_of(k * w, w), w)

    def forward_chunk(k, carry):
        both = dot_nt(xs[...], fhi[lines_of(k), :])
        p[k] = both[:rows] + both[rows:] + dot_nt(xs[:rows, :], flo[lines_of(k), :])

        @pl.when(z == 0)
        def _():
            to_right(p, k).start()

        @pl.when(z == nb - 1)
        def _():
            to_left(p, k).start()

        relay(k)
        return carry

    lax.fori_loop(0, kc, forward_chunk, 0)

    def slopes(k):
        tot[...] = p[k]

        @pl.when(z > 0)
        def _():
            tot[...] += r_left[k]

        @pl.when(z < nb - 1)
        def _():
            tot[...] += r_right[k]

        at = pl.ds(pl.multiple_of(c * lc + k * w, w), w)
        flow_out[:, at] = tot[pl.ds(pl.multiple_of((c * nb + z) * r, r), r), :]
        for dc in range(1, ns):
            other = lax.rem(c + dc, ns)
            fsend[dc - 1, :, lines_of(k)] = tot[pl.ds(pl.multiple_of((other * nb + z) * r, r), r), :]
        limits = lim[c * kc + k].astype(F32) / 100.0
        t = tot[...]
        slope = 2.0 * cost[c * kc + k] * (
            jnp.maximum(t - limits, 0.0) - jnp.maximum(-t - limits, 0.0)
        )
        high, low = split(slope)
        ss[:rows, :] = high
        ss[rows:, :] = low

    def backward_tile(k, col):
        cols = pl.ds(col, tw)
        both = dot_nn(ss[...], fhi[lines_of(k), cols])
        g[:, cols] += both[:rows] + both[rows:] + dot_nn(ss[:rows, :], flo[lines_of(k), cols])

    def backward_chunk(k, carry):
        relay(kc + k)
        slopes(k)

        def tile(t, carry2):
            backward_tile(k, pl.multiple_of(t * tw, tw))
            return carry2

        lax.fori_loop(0, nl * nt, tile, 0)
        return carry

    lax.fori_loop(0, kc - 1, backward_chunk, 0)
    last = kc - 1
    relay(jnp.int32(kc + last))
    slopes(last)

    def flows_over(dc):
        return remote(
            fsend.at[dc - 1], frecv.at[dc - 1], f_send.at[dc - 1], f_recv.at[dc - 1],
            {"scen": lax.rem(c + dc, ns)},
        )

    for dc in range(1, ns):
        flows_over(dc).start()

    order = [(dx, t) for dx in range(1, nl + 1) for t in range(nt)]

    def column(dx, t):
        return pl.multiple_of(lax.rem(x + dx, nl) * bx + t * tw, tw)

    def grad_core(i, dc):
        cols = pl.ds(column(*order[i]), tw)
        other = lax.rem(c + dc, ns)
        return remote(
            g.at[pl.ds(pl.multiple_of(other * own_rows, own_rows), own_rows), cols],
            gc.at[dc - 1, :, cols], gc_send.at[dc - 1, i], gc_recv.at[dc - 1, i], {"scen": other},
        )

    def grad_line(dx, t):
        cols = pl.ds(t * tw, tw)
        return remote(
            hs.at[dx - 1, :, cols], hx.at[dx - 1, :, cols],
            hx_send.at[dx - 1, t], hx_recv.at[dx - 1, t], {"line": lax.rem(x + dx, nl)},
        )

    def grad_bus(d, t):
        cols = pl.ds(t * tw, tw)
        to = lax.rem(z + d, nb)
        return remote(
            own.at[pl.ds(pl.multiple_of(to * r, r), r), cols],
            gout.at[pl.ds(pl.multiple_of(z * r, r), r), cols],
            go_send.at[d - 1, t], go_recv.at[d - 1, t], {"bus": to},
        )

    for i, (dx, t) in enumerate(order):
        backward_tile(last, column(dx, t))
        for dc in range(1, ns):
            grad_core(i, dc).start()

    mine = pl.ds(pl.multiple_of(c * own_rows, own_rows), own_rows)
    for i, (dx, t) in enumerate(order):
        cols = pl.ds(column(dx, t), tw)
        total = g[mine, cols]
        for dc in range(1, ns):
            grad_core(i, dc).wait_recv()
            total = total + gc[dc - 1, :, cols]
        if dx < nl:
            hs[dx - 1, :, t * tw:(t + 1) * tw] = total
            grad_line(dx, t).start()
        else:
            for e in range(1, nl):
                grad_line(e, t).wait_recv()
                total = total + hx[e - 1, :, t * tw:(t + 1) * tw]
            own[:, t * tw:(t + 1) * tw] = total
            for d in range(1, nb):
                grad_bus(d, t).start()

    for dc in range(1, ns):
        flows_over(dc).wait_recv()
        sender = lax.rem(c + ns - dc, ns)
        flow_out[:, pl.ds(pl.multiple_of(sender * lc, lc), lc)] = frecv[dc - 1]

    here = pl.ds(pl.multiple_of(z * r, r), r)
    gout[here, :] = own[here, :]

    for d in range(1, nb):
        over_bus(d).wait_send()
    for d in range(nb):
        for dx in range(1, nl):
            over_line(dx, d).wait_send()
        for dx in range(nl):
            for dc in range(1, ns):
                over_core(dx, d, dc).wait_send()

    def sent(k, carry):
        @pl.when(z < nb - 1)
        def _():
            to_right(p, k).wait_send()

        @pl.when(z > 0)
        def _():
            to_left(p, k).wait_send()

        return carry

    lax.fori_loop(0, kc, sent, 0)
    for dc in range(1, ns):
        flows_over(dc).wait_send()
        for i in range(len(order)):
            grad_core(i, dc).wait_send()
    for t in range(nt):
        for dx in range(1, nl):
            grad_line(dx, t).wait_send()
        for d in range(1, nb):
            grad_bus(d, t).wait_recv()
            grad_bus(d, t).wait_send()
    for k in range(nb):
        grad_out[:, k, :] = gout[k * r:(k + 1) * r, :]


def on_device(sizes, injections, shift_factors, line_limits, overload_cost):
    nb, nl, ns = sizes
    r, _, bx = injections.shape
    lines, buses = shift_factors.shape
    lc = lines // ns
    w = max(128, lc // 8)
    ch = w // 2
    nbuf = 4
    tw = max(128, bx // 2)
    kc, nt = lc // w, bx // tw
    own_rows = nb * r
    rows = ns * own_rows
    dims = (nb, nl, ns, r, bx, lc, w, ch, nbuf, tw)
    vmem, dma = pltpu.VMEM, pltpu.SemaphoreType.DMA
    whole = pl.BlockSpec(memory_space=pltpu.VMEM)
    return pl.pallas_call(
        functools.partial(kernel, dims),
        out_shape=(
            jax.ShapeDtypeStruct((r, lines), F32),
            jax.ShapeDtypeStruct((r, nb, bx), F32),
        ),
        in_specs=[whole, whole, whole, pl.BlockSpec(memory_space=pl.ANY)],
        out_specs=(whole, whole),
        scratch_shapes=[
            vmem((nb, r, bx), F32),
            vmem((nl, rows, bx), F32),
            vmem((2 * rows, buses), BF16),
            vmem((nbuf, ch, buses), F32),
            vmem((lc, buses), BF16),
            vmem((lc, buses), BF16),
            vmem((kc, rows, w), F32),
            vmem((kc, rows, w), F32),
            vmem((kc, rows, w), F32),
            vmem((kc, rows, w), F32),
            vmem((kc, rows, w), F32),
            vmem((rows, w), F32),
            vmem((2 * rows, w), BF16),
            vmem((ns - 1, r, lc), F32),
            vmem((ns - 1, r, lc), F32),
            vmem((rows, buses), F32),
            vmem((ns - 1, own_rows, buses), F32),
            vmem((nl - 1, own_rows, bx), F32),
            vmem((nl - 1, own_rows, bx), F32),
            vmem((own_rows, bx), F32),
            vmem((own_rows, bx), F32),
            dma((nbuf,)),
            dma((nb,)),
            dma((nl, nb)),
            dma((nl, nb, ns)),
            dma((nl, nb, ns)),
            dma((kc,)),
            dma((kc,)),
            dma((kc,)),
            dma((kc,)),
            dma((ns - 1,)),
            dma((ns - 1,)),
            dma((ns - 1, nl * nt)),
            dma((ns - 1, nl * nt)),
            dma((nl - 1, nt)),
            dma((nl - 1, nt)),
            dma((nb - 1, nt)),
            dma((nb - 1, nt)),
        ],
        compiler_params=pltpu.CompilerParams(
            collective_id=0, has_side_effects=True, vmem_limit_bytes=58 * 1024 * 1024
        ),
        cost_estimate=pl.CostEstimate(
            flops=12 * rows * lc * buses, bytes_accessed=4 * lc * buses, transcendentals=0
        ),
    )(
        injections,
        line_limits.reshape(ns * kc, 1, w),
        overload_cost.reshape(ns * kc, 1, w),
        shift_factors,
    )


def solution(mesh):
    sizes = tuple(mesh.shape[a] for a in ("bus", "line", "scen"))
    in_specs = (P(("grp", "bus", "scen"), None, "line"), P("line", "bus"), P("line"), P("line"))
    out_specs = (P(("grp", "bus", "scen"), "line"), P(("grp", "bus", "scen"), None, "line"))
    return jax.shard_map(
        functools.partial(on_device, sizes),
        mesh=mesh, in_specs=in_specs, out_specs=out_specs, check_vma=False,
    )
```

```python
import functools

import jax
import jax.numpy as jnp
from jax import lax
from jax.experimental import pallas as pl
from jax.experimental.pallas import tpu as pltpu
from jax.sharding import PartitionSpec as P

MESH = pl.DeviceIdType.MESH
F32 = jnp.float32
BF16 = jnp.bfloat16


def split(value):
    high = value.astype(BF16)
    return high, (value - high.astype(F32)).astype(BF16)


def dot_nt(a, b):
    return lax.dot_general(a, b, (((1,), (1,)), ((), ())), preferred_element_type=F32)


def dot_nn(a, b):
    return jnp.dot(a, b, preferred_element_type=F32)


def kernel(
    dims, inj, lim, cost, fac, flow_out, grad_out,
    snd, xbuf, xs, stage, fhi, flo, p, s_right, s_left, r_left, r_right,
    tot, ss, fsend, frecv, g, gc, hs, hx, own, gout,
    ld_sem, z_send, x_send, c_send, b_recv, right_send, left_send, left_recv, right_recv,
    f_send, f_recv, gc_send, gc_recv, hx_send, hx_recv, go_send, go_recv,
):
    nb, nl, ns, r, bx, lc, w, ch, nbuf, tw, bt = dims
    z, x, c = lax.axis_index("bus"), lax.axis_index("line"), lax.axis_index("scen")
    kc, nch, nt = lc // w, lc // ch, bx // tw
    own_rows = nb * r
    rows = ns * own_rows

    def remote(src, dst, send, recv, where):
        return pltpu.make_async_remote_copy(
            src_ref=src, dst_ref=dst, send_sem=send, recv_sem=recv,
            device_id=where, device_id_type=MESH,
        )

    def load(i):
        start = pl.multiple_of(c * lc + i * ch, ch)
        slot = lax.rem(i, nbuf)
        return pltpu.make_async_copy(fac.at[pl.ds(start, ch), :], stage.at[slot], ld_sem.at[slot])

    for i in range(min(nbuf, nch)):
        load(jnp.int32(i)).start()

    barrier = pltpu.get_barrier_semaphore()
    for axis, here, count in (("bus", z, nb), ("line", x, nl), ("scen", c, ns)):
        for d in range(1, count):
            pl.semaphore_signal(
                barrier, inc=1, device_id={axis: lax.rem(here + d, count)}, device_id_type=MESH
            )

    for k in range(nb):
        snd[k] = inj[:, k, :]
    g[...] = jnp.zeros_like(g)
    pl.semaphore_wait(barrier, nb + nl + ns - 3)

    def block(xh, zz, cc):
        return xbuf.at[xh, pl.ds(pl.multiple_of((cc * nb + zz) * r, r), r), :]

    def over_bus(d):
        to = lax.rem(z + d, nb)
        return remote(snd.at[to], block(x, z, c), z_send.at[d], b_recv.at[x, z, c], {"bus": to})

    def over_line(dx, d):
        zz = lax.rem(z + nb - d, nb)
        return remote(
            block(x, zz, c), block(x, zz, c), x_send.at[dx, d], b_recv.at[x, zz, c],
            {"line": lax.rem(x + dx, nl)},
        )

    def over_core(dx, d, dc):
        zz, xh = lax.rem(z + nb - d, nb), lax.rem(x + nl - dx, nl)
        return remote(
            block(xh, zz, c), block(xh, zz, c), c_send.at[dx, d, dc], b_recv.at[xh, zz, c],
            {"scen": lax.rem(c + dc, ns)},
        )

    def arrived(xh, zz, cc):
        remote(
            block(xh, zz, cc), block(xh, zz, cc), z_send.at[0], b_recv.at[xh, zz, cc],
            {"bus": lax.rem(z + 1, nb)},
        ).wait_recv()

    for d in range(1, nb):
        over_bus(d).start()
    start_row = pl.multiple_of((c * nb + z) * r, r)
    xbuf[x, pl.ds(start_row, r), :] = snd[z]

    def forward(d):
        for dx in range(1, nl):
            over_line(dx, d).start()
        for dc in range(1, ns):
            over_core(0, d, dc).start()

    forward(0)

    def convert(i, carry):
        load(i).wait()
        slot = lax.rem(i, nbuf)
        high, low = split(stage[slot])
        at = pl.ds(pl.multiple_of(i * ch, ch), ch)
        fhi[at, :] = high
        flo[at, :] = low

        @pl.when(i + nbuf < nch)
        def _():
            load(i + nbuf).start()

        return carry

    def forward_line(d):
        for dx in range(1, nl):
            arrived(lax.rem(x + nl - dx, nl), lax.rem(z + nb - d, nb), c)
            for dc in range(1, ns):
                over_core(dx, d, dc).start()

    def take(xh):
        for dc in range(1, ns):
            for d in range(nb):
                arrived(xh, lax.rem(z + nb - d, nb), lax.rem(c + dc, ns))
        cols = half(xh)
        high, low = split(xbuf[xh])
        xs[:rows, cols] = high
        xs[rows:, cols] = low

    def half(xh):
        return pl.ds(pl.multiple_of(xh * bx, bx), bx)

    def lines_of(k):
        return pl.ds(pl.multiple_of(k * w, w), w)

    def product(k, xh):
        cols = half(xh)
        both = dot_nt(xs[:, cols], fhi[lines_of(k), cols])
        return both[:rows] + both[rows:] + dot_nt(xs[:rows, cols], flo[lines_of(k), cols])

    def own_half(k, carry):
        p[k] = product(k, x)
        return carry

    for n in range(1, nb + 1):
        lax.fori_loop((n - 1) * nch // nb, n * nch // nb, convert, 0)
        if n < nb:
            arrived(x, lax.rem(z + nb - n, nb), c)
            forward(n)
            forward_line(n - 1)
    take(x)
    lax.fori_loop(0, 1, own_half, 0)
    forward_line(nb - 1)
    lax.fori_loop(1, kc, own_half, 0)
    for dx in range(1, nl):
        take(lax.rem(x + dx, nl))

    def to_right(src, k):
        return remote(
            src.at[k], r_left.at[k], right_send.at[k], left_recv.at[k],
            {"bus": lax.rem(z + 1, nb)},
        )

    def to_left(src, k):
        return remote(
            src.at[k], r_right.at[k], left_send.at[k], right_recv.at[k],
            {"bus": lax.rem(z + nb - 1, nb)},
        )

    lag_left, lag_right = 2 * z, 2 * (nb - 1 - z)
    lag = jnp.maximum(lag_left, lag_right)

    def relay(s):
        k = s - lag_left

        @pl.when((z > 0) & (k >= 0) & (k < kc))
        def _():
            to_right(s_right, k).wait_recv()

            @pl.when(z < nb - 1)
            def _():
                s_right[k] = r_left[k] + p[k]
                to_right(s_right, k).start()

        m = s - lag_right

        @pl.when((z < nb - 1) & (m >= 0) & (m < kc))
        def _():
            to_left(s_left, m).wait_recv()

            @pl.when(z > 0)
            def _():
                s_left[m] = r_right[m] + p[m]
                to_left(s_left, m).start()

    def forward_chunk(k):
        for dx in range(1, nl):
            p[k] += product(k, lax.rem(x + dx, nl))

        @pl.when(z == 0)
        def _():
            to_right(p, k).start()

        @pl.when(z == nb - 1)
        def _():
            to_left(p, k).start()

    def slopes(k):
        tot[...] = p[k]

        @pl.when(z > 0)
        def _():
            tot[...] += r_left[k]

        @pl.when(z < nb - 1)
        def _():
            tot[...] += r_right[k]

        at = pl.ds(pl.multiple_of(c * lc + k * w, w), w)
        flow_out[:, at] = tot[pl.ds(pl.multiple_of((c * nb + z) * r, r), r), :]
        for dc in range(1, ns):
            other = lax.rem(c + dc, ns)
            fsend[dc - 1, :, lines_of(k)] = tot[pl.ds(pl.multiple_of((other * nb + z) * r, r), r), :]
        limits = lim[c * kc + k].astype(F32) / 100.0
        t = tot[...]
        slope = 2.0 * cost[c * kc + k] * (
            jnp.maximum(t - limits, 0.0) - jnp.maximum(-t - limits, 0.0)
        )
        high, low = split(slope)
        ss[:rows, :] = high
        ss[rows:, :] = low

    def backward_tile(k, col, width):
        cols = pl.ds(col, width)
        both = dot_nn(ss[...], fhi[lines_of(k), cols])
        g[:, cols] += both[:rows] + both[rows:] + dot_nn(ss[:rows, :], flo[lines_of(k), cols])

    last = kc - 1

    def step(s, carry):
        @pl.when(2 * s < kc)
        def _():
            forward_chunk(2 * s)
            forward_chunk(2 * s + 1)

        relay(s)
        k = s - lag

        @pl.when((k >= 0) & (k < last))
        def _():
            slopes(k)

            def tile(t, carry2):
                backward_tile(k, pl.multiple_of(t * bt, bt), bt)
                return carry2

            lax.fori_loop(0, nl * bx // bt, tile, 0)

        return carry

    lax.fori_loop(0, kc + 2 * (nb - 1), step, 0)
    slopes(last)

    def flows_over(dc):
        return remote(
            fsend.at[dc - 1], frecv.at[dc - 1], f_send.at[dc - 1], f_recv.at[dc - 1],
            {"scen": lax.rem(c + dc, ns)},
        )

    for dc in range(1, ns):
        flows_over(dc).start()

    order = [(dx, t) for dx in range(1, nl + 1) for t in range(nt)]

    def column(dx, t):
        return pl.multiple_of(lax.rem(x + dx, nl) * bx + t * tw, tw)

    def grad_core(i, dc):
        cols = pl.ds(column(*order[i]), tw)
        other = lax.rem(c + dc, ns)
        return remote(
            g.at[pl.ds(pl.multiple_of(other * own_rows, own_rows), own_rows), cols],
            gc.at[dc - 1, :, cols], gc_send.at[dc - 1, i], gc_recv.at[dc - 1, i], {"scen": other},
        )

    def grad_line(dx, t):
        cols = pl.ds(t * tw, tw)
        return remote(
            hs.at[dx - 1, :, cols], hx.at[dx - 1, :, cols],
            hx_send.at[dx - 1, t], hx_recv.at[dx - 1, t], {"line": lax.rem(x + dx, nl)},
        )

    def grad_bus(d, t):
        cols = pl.ds(t * tw, tw)
        to = lax.rem(z + d, nb)
        return remote(
            own.at[pl.ds(pl.multiple_of(to * r, r), r), cols],
            gout.at[pl.ds(pl.multiple_of(z * r, r), r), cols],
            go_send.at[d - 1, t], go_recv.at[d - 1, t], {"bus": to},
        )

    for i, (dx, t) in enumerate(order):
        backward_tile(last, column(dx, t), tw)
        for dc in range(1, ns):
            grad_core(i, dc).start()

    mine = pl.ds(pl.multiple_of(c * own_rows, own_rows), own_rows)
    for i, (dx, t) in enumerate(order):
        cols = pl.ds(column(dx, t), tw)
        total = g[mine, cols]
        for dc in range(1, ns):
            grad_core(i, dc).wait_recv()
            total = total + gc[dc - 1, :, cols]
        if dx < nl:
            hs[dx - 1, :, t * tw:(t + 1) * tw] = total
            grad_line(dx, t).start()
        else:
            for e in range(1, nl):
                grad_line(e, t).wait_recv()
                total = total + hx[e - 1, :, t * tw:(t + 1) * tw]
            own[:, t * tw:(t + 1) * tw] = total
            for d in range(1, nb):
                grad_bus(d, t).start()

    for dc in range(1, ns):
        flows_over(dc).wait_recv()
        sender = lax.rem(c + ns - dc, ns)
        flow_out[:, pl.ds(pl.multiple_of(sender * lc, lc), lc)] = frecv[dc - 1]

    here = pl.ds(pl.multiple_of(z * r, r), r)
    gout[here, :] = own[here, :]

    for d in range(1, nb):
        over_bus(d).wait_send()
    for d in range(nb):
        for dx in range(1, nl):
            over_line(dx, d).wait_send()
        for dx in range(nl):
            for dc in range(1, ns):
                over_core(dx, d, dc).wait_send()

    def sent(k, carry):
        @pl.when(z < nb - 1)
        def _():
            to_right(p, k).wait_send()

        @pl.when(z > 0)
        def _():
            to_left(p, k).wait_send()

        return carry

    lax.fori_loop(0, kc, sent, 0)
    for dc in range(1, ns):
        flows_over(dc).wait_send()
        for i in range(len(order)):
            grad_core(i, dc).wait_send()
    for t in range(nt):
        for dx in range(1, nl):
            grad_line(dx, t).wait_send()
        for d in range(1, nb):
            grad_bus(d, t).wait_recv()
            grad_bus(d, t).wait_send()
    for k in range(nb):
        grad_out[:, k, :] = gout[k * r:(k + 1) * r, :]


def on_device(sizes, injections, shift_factors, line_limits, overload_cost):
    nb, nl, ns = sizes
    r, _, bx = injections.shape
    lines, buses = shift_factors.shape
    lc = lines // ns
    w = max(128, lc // 8)
    ch = w // 2
    nbuf = 8
    tw = max(128, bx // 4)
    bt = max(128, bx // 2)
    kc, nt = lc // w, bx // tw
    own_rows = nb * r
    rows = ns * own_rows
    dims = (nb, nl, ns, r, bx, lc, w, ch, nbuf, tw, bt)
    vmem, dma = pltpu.VMEM, pltpu.SemaphoreType.DMA
    whole = pl.BlockSpec(memory_space=pltpu.VMEM)
    return pl.pallas_call(
        functools.partial(kernel, dims),
        out_shape=(
            jax.ShapeDtypeStruct((r, lines), F32),
            jax.ShapeDtypeStruct((r, nb, bx), F32),
        ),
        in_specs=[whole, whole, whole, pl.BlockSpec(memory_space=pl.ANY)],
        out_specs=(whole, whole),
        scratch_shapes=[
            vmem((nb, r, bx), F32),
            vmem((nl, rows, bx), F32),
            vmem((2 * rows, buses), BF16),
            vmem((nbuf, ch, buses), F32),
            vmem((lc, buses), BF16),
            vmem((lc, buses), BF16),
            vmem((kc, rows, w), F32),
            vmem((kc, rows, w), F32),
            vmem((kc, rows, w), F32),
            vmem((kc, rows, w), F32),
            vmem((kc, rows, w), F32),
            vmem((rows, w), F32),
            vmem((2 * rows, w), BF16),
            vmem((ns - 1, r, lc), F32),
            vmem((ns - 1, r, lc), F32),
            vmem((rows, buses), F32),
            vmem((ns - 1, own_rows, buses), F32),
            vmem((nl - 1, own_rows, bx), F32),
            vmem((nl - 1, own_rows, bx), F32),
            vmem((own_rows, bx), F32),
            vmem((own_rows, bx), F32),
            dma((nbuf,)),
            dma((nb,)),
            dma((nl, nb)),
            dma((nl, nb, ns)),
            dma((nl, nb, ns)),
            dma((kc,)),
            dma((kc,)),
            dma((kc,)),
            dma((kc,)),
            dma((ns - 1,)),
            dma((ns - 1,)),
            dma((ns - 1, nl * nt)),
            dma((ns - 1, nl * nt)),
            dma((nl - 1, nt)),
            dma((nl - 1, nt)),
            dma((nb - 1, nt)),
            dma((nb - 1, nt)),
        ],
        compiler_params=pltpu.CompilerParams(
            collective_id=0, has_side_effects=True, vmem_limit_bytes=60 * 1024 * 1024
        ),
        cost_estimate=pl.CostEstimate(
            flops=12 * rows * lc * buses, bytes_accessed=4 * lc * buses, transcendentals=0
        ),
    )(
        injections,
        line_limits.reshape(ns * kc, 1, w),
        overload_cost.reshape(ns * kc, 1, w),
        shift_factors,
    )


def solution(mesh):
    sizes = tuple(mesh.shape[a] for a in ("bus", "line", "scen"))
    in_specs = (P(("grp", "bus", "scen"), None, "line"), P("line", "bus"), P("line"), P("line"))
    out_specs = (P(("grp", "bus", "scen"), "line"), P(("grp", "bus", "scen"), None, "line"))
    return jax.shard_map(
        functools.partial(on_device, sizes),
        mesh=mesh, in_specs=in_specs, out_specs=out_specs, check_vma=False,
    )
```

```python
import functools

import jax
import jax.numpy as jnp
from jax import lax
from jax.experimental import pallas as pl
from jax.experimental.pallas import tpu as pltpu
from jax.sharding import PartitionSpec as P

MESH = pl.DeviceIdType.MESH
F32 = jnp.float32
BF16 = jnp.bfloat16


def split(value):
    high = value.astype(BF16)
    return high, (value - high.astype(F32)).astype(BF16)


def dot_nt(a, b):
    return lax.dot_general(a, b, (((1,), (1,)), ((), ())), preferred_element_type=F32)


def dot_nn(a, b):
    return jnp.dot(a, b, preferred_element_type=F32)


def kernel(
    dims, inj, lim, cost, fac, flow_out, grad_out,
    snd, xbuf, xs, stage, fhi, flo, p, s_right, s_left, r_left, r_right,
    tot, ss, fsend, frecv, g, gc, hs, hx, own, gout,
    ld_sem, z_send, x_send, c_send, b_recv, right_send, left_send, left_recv, right_recv,
    f_send, f_recv, gc_send, gc_recv, hx_send, hx_recv, go_send, go_recv,
):
    nb, nl, ns, r, bx, lc, w, ch, nbuf, tw, bt = dims
    z, x, c = lax.axis_index("bus"), lax.axis_index("line"), lax.axis_index("scen")
    kc, nch, nt = lc // w, lc // ch, bx // tw
    own_rows = nb * r
    rows = ns * own_rows

    def remote(src, dst, send, recv, where):
        return pltpu.make_async_remote_copy(
            src_ref=src, dst_ref=dst, send_sem=send, recv_sem=recv,
            device_id=where, device_id_type=MESH,
        )

    def load(i):
        start = pl.multiple_of(c * lc + i * ch, ch)
        slot = lax.rem(i, nbuf)
        return pltpu.make_async_copy(fac.at[pl.ds(start, ch), :], stage.at[slot], ld_sem.at[slot])

    for i in range(min(nbuf, nch)):
        load(jnp.int32(i)).start()

    barrier = pltpu.get_barrier_semaphore()
    for axis, here, count in (("bus", z, nb), ("line", x, nl), ("scen", c, ns)):
        for d in range(1, count):
            pl.semaphore_signal(
                barrier, inc=1, device_id={axis: lax.rem(here + d, count)}, device_id_type=MESH
            )

    for k in range(nb):
        snd[k] = inj[:, k, :]
    g[...] = jnp.zeros_like(g)
    pl.semaphore_wait(barrier, nb + nl + ns - 3)

    def block(xh, zz, cc):
        return xbuf.at[xh, pl.ds(pl.multiple_of((cc * nb + zz) * r, r), r), :]

    def over_bus(d):
        to = lax.rem(z + d, nb)
        return remote(snd.at[to], block(x, z, c), z_send.at[d], b_recv.at[x, z, c], {"bus": to})

    def over_line(dx, d):
        zz = lax.rem(z + nb - d, nb)
        return remote(
            block(x, zz, c), block(x, zz, c), x_send.at[dx, d], b_recv.at[x, zz, c],
            {"line": lax.rem(x + dx, nl)},
        )

    def over_core(dx, d, dc):
        zz, xh = lax.rem(z + nb - d, nb), lax.rem(x + nl - dx, nl)
        return remote(
            block(xh, zz, c), block(xh, zz, c), c_send.at[dx, d, dc], b_recv.at[xh, zz, c],
            {"scen": lax.rem(c + dc, ns)},
        )

    def arrived(xh, zz, cc):
        remote(
            block(xh, zz, cc), block(xh, zz, cc), z_send.at[0], b_recv.at[xh, zz, cc],
            {"bus": lax.rem(z + 1, nb)},
        ).wait_recv()

    for d in range(1, nb):
        over_bus(d).start()
    start_row = pl.multiple_of((c * nb + z) * r, r)
    xbuf[x, pl.ds(start_row, r), :] = snd[z]

    def forward(d):
        for dx in range(1, nl):
            over_line(dx, d).start()
        for dc in range(1, ns):
            over_core(0, d, dc).start()

    forward(0)

    def convert(i, carry):
        load(i).wait()
        slot = lax.rem(i, nbuf)
        high, low = split(stage[slot])
        at = pl.ds(pl.multiple_of(i * ch, ch), ch)
        fhi[at, :] = high
        flo[at, :] = low

        @pl.when(i + nbuf < nch)
        def _():
            load(i + nbuf).start()

        return carry

    def forward_line(d):
        for dx in range(1, nl):
            arrived(lax.rem(x + nl - dx, nl), lax.rem(z + nb - d, nb), c)
            for dc in range(1, ns):
                over_core(dx, d, dc).start()

    def take(xh):
        for dc in range(1, ns):
            for d in range(nb):
                arrived(xh, lax.rem(z + nb - d, nb), lax.rem(c + dc, ns))
        cols = half(xh)
        high, low = split(xbuf[xh])
        xs[:rows, cols] = high
        xs[rows:, cols] = low

    def half(xh):
        return pl.ds(pl.multiple_of(xh * bx, bx), bx)

    def lines_of(k):
        return pl.ds(pl.multiple_of(k * w, w), w)

    def product(k, xh):
        cols = half(xh)
        both = dot_nt(xs[:, cols], fhi[lines_of(k), cols])
        return both[:rows] + both[rows:] + dot_nt(xs[:rows, cols], flo[lines_of(k), cols])

    hr = rows // 2

    def put(k, value):
        p[2 * k] = value[:hr]
        p[2 * k + 1] = value[hr:]

    def own_half(k, carry):
        put(k, product(k, x))
        return carry

    for n in range(1, nb + 1):
        lax.fori_loop((n - 1) * nch // nb, n * nch // nb, convert, 0)
        if n < nb:
            arrived(x, lax.rem(z + nb - n, nb), c)
            forward(n)
            forward_line(n - 1)
    take(x)
    first = kc // 2
    lax.fori_loop(first, first + 1, own_half, 0)
    forward_line(nb - 1)
    lax.fori_loop(first + 1, kc, own_half, 0)
    for dx in range(1, nl):
        take(lax.rem(x + dx, nl))

    def to_right(src, k):
        return remote(
            src.at[k], r_left.at[k], right_send.at[k], left_recv.at[k],
            {"bus": lax.rem(z + 1, nb)},
        )

    def to_left(src, k):
        return remote(
            src.at[k], r_right.at[k], left_send.at[k], right_recv.at[k],
            {"bus": lax.rem(z + nb - 1, nb)},
        )

    lag_left = jnp.where(z == nb - 1, kc, jnp.minimum(2 * z, kc))
    lag_right = jnp.where(z == 0, kc, jnp.minimum(2 * (nb - 1 - z), kc))

    def relay(s):
        k = s - lag_left

        @pl.when((z > 0) & (k >= 0) & (k < kc))
        def _():
            for h in range(2):
                i = 2 * k + h
                to_right(s_right, i).wait_recv()

                @pl.when(z < nb - 1)
                def _():
                    s_right[i] = r_left[i] + p[i]
                    to_right(s_right, i).start()

        m = s - lag_right

        @pl.when((z < nb - 1) & (m >= 0) & (m < kc))
        def _():
            for h in range(2):
                i = 2 * m + h
                to_left(s_left, i).wait_recv()

                @pl.when(z > 0)
                def _():
                    s_left[i] = r_right[i] + p[i]
                    to_left(s_left, i).start()

    def send_ends(k):
        for h in range(2):
            @pl.when(z == 0)
            def _():
                to_right(p, 2 * k + h).start()

            @pl.when(z == nb - 1)
            def _():
                to_left(p, 2 * k + h).start()

    def whole_chunk(k, carry):
        both = dot_nt(xs[...], fhi[lines_of(k), :])
        put(k, both[:rows] + both[rows:] + dot_nt(xs[:rows, :], flo[lines_of(k), :]))
        send_ends(k)
        relay(k)
        return carry

    def rest_chunk(k, carry):
        for dx in range(1, nl):
            value = product(k, lax.rem(x + dx, nl))
            p[2 * k] += value[:hr]
            p[2 * k + 1] += value[hr:]
        send_ends(k)
        relay(k)
        return carry

    lax.fori_loop(0, first, whole_chunk, 0)
    lax.fori_loop(first, kc, rest_chunk, 0)

    def slopes(k):
        for h in range(2):
            i = 2 * k + h
            part = pl.ds(h * hr, hr)
            tot[part, :] = p[i]

            @pl.when(z > 0)
            def _():
                tot[part, :] += r_left[i]

            @pl.when(z < nb - 1)
            def _():
                tot[part, :] += r_right[i]

        at = pl.ds(pl.multiple_of(c * lc + k * w, w), w)
        flow_out[:, at] = tot[pl.ds(pl.multiple_of((c * nb + z) * r, r), r), :]
        for dc in range(1, ns):
            other = lax.rem(c + dc, ns)
            fsend[dc - 1, :, lines_of(k)] = tot[pl.ds(pl.multiple_of((other * nb + z) * r, r), r), :]
        limits = lim[c * kc + k].astype(F32) / 100.0
        t = tot[...]
        slope = 2.0 * cost[c * kc + k] * (
            jnp.maximum(t - limits, 0.0) - jnp.maximum(-t - limits, 0.0)
        )
        high, low = split(slope)
        ss[:rows, :] = high
        ss[rows:, :] = low

    def backward_tile(k, col, width):
        cols = pl.ds(col, width)
        both = dot_nn(ss[...], fhi[lines_of(k), cols])
        g[:, cols] += both[:rows] + both[rows:] + dot_nn(ss[:rows, :], flo[lines_of(k), cols])

    last = kc - 1

    def backward_chunk(k, carry):
        relay(kc + k)
        slopes(k)

        def tile(t, carry2):
            backward_tile(k, pl.multiple_of(t * bt, bt), bt)
            return carry2

        lax.fori_loop(0, nl * bx // bt, tile, 0)
        return carry

    lax.fori_loop(0, last, backward_chunk, 0)
    relay(jnp.int32(kc + last))
    slopes(last)

    def flows_over(dc):
        return remote(
            fsend.at[dc - 1], frecv.at[dc - 1], f_send.at[dc - 1], f_recv.at[dc - 1],
            {"scen": lax.rem(c + dc, ns)},
        )

    for dc in range(1, ns):
        flows_over(dc).start()

    order = [(dx, t) for dx in range(1, nl + 1) for t in range(nt)]

    def column(dx, t):
        return pl.multiple_of(lax.rem(x + dx, nl) * bx + t * tw, tw)

    def grad_core(i, dc):
        cols = pl.ds(column(*order[i]), tw)
        other = lax.rem(c + dc, ns)
        return remote(
            g.at[pl.ds(pl.multiple_of(other * own_rows, own_rows), own_rows), cols],
            gc.at[dc - 1, :, cols], gc_send.at[dc - 1, i], gc_recv.at[dc - 1, i], {"scen": other},
        )

    def grad_line(dx, t):
        cols = pl.ds(t * tw, tw)
        return remote(
            hs.at[dx - 1, :, cols], hx.at[dx - 1, :, cols],
            hx_send.at[dx - 1, t], hx_recv.at[dx - 1, t], {"line": lax.rem(x + dx, nl)},
        )

    def grad_bus(d, t):
        cols = pl.ds(t * tw, tw)
        to = lax.rem(z + d, nb)
        return remote(
            own.at[pl.ds(pl.multiple_of(to * r, r), r), cols],
            gout.at[pl.ds(pl.multiple_of(z * r, r), r), cols],
            go_send.at[d - 1, t], go_recv.at[d - 1, t], {"bus": to},
        )

    for i, (dx, t) in enumerate(order):
        backward_tile(last, column(dx, t), tw)
        for dc in range(1, ns):
            grad_core(i, dc).start()

    mine = pl.ds(pl.multiple_of(c * own_rows, own_rows), own_rows)
    for i, (dx, t) in enumerate(order):
        cols = pl.ds(column(dx, t), tw)
        total = g[mine, cols]
        for dc in range(1, ns):
            grad_core(i, dc).wait_recv()
            total = total + gc[dc - 1, :, cols]
        if dx < nl:
            hs[dx - 1, :, t * tw:(t + 1) * tw] = total
            grad_line(dx, t).start()
        else:
            for e in range(1, nl):
                grad_line(e, t).wait_recv()
                total = total + hx[e - 1, :, t * tw:(t + 1) * tw]
            own[:, t * tw:(t + 1) * tw] = total
            for d in range(1, nb):
                grad_bus(d, t).start()

    for dc in range(1, ns):
        flows_over(dc).wait_recv()
        sender = lax.rem(c + ns - dc, ns)
        flow_out[:, pl.ds(pl.multiple_of(sender * lc, lc), lc)] = frecv[dc - 1]

    here = pl.ds(pl.multiple_of(z * r, r), r)
    gout[here, :] = own[here, :]

    for d in range(1, nb):
        over_bus(d).wait_send()
    for d in range(nb):
        for dx in range(1, nl):
            over_line(dx, d).wait_send()
        for dx in range(nl):
            for dc in range(1, ns):
                over_core(dx, d, dc).wait_send()

    def sent(k, carry):
        @pl.when(z < nb - 1)
        def _():
            to_right(p, k).wait_send()

        @pl.when(z > 0)
        def _():
            to_left(p, k).wait_send()

        return carry

    lax.fori_loop(0, 2 * kc, sent, 0)
    for dc in range(1, ns):
        flows_over(dc).wait_send()
        for i in range(len(order)):
            grad_core(i, dc).wait_send()
    for t in range(nt):
        for dx in range(1, nl):
            grad_line(dx, t).wait_send()
        for d in range(1, nb):
            grad_bus(d, t).wait_recv()
            grad_bus(d, t).wait_send()
    for k in range(nb):
        grad_out[:, k, :] = gout[k * r:(k + 1) * r, :]


def hand_on(flows, grads, flows_out, grads_out, sem):
    first = pltpu.make_async_copy(flows, flows_out, sem.at[0])
    second = pltpu.make_async_copy(grads, grads_out, sem.at[1])
    first.start()
    second.start()
    first.wait()
    second.wait()


def on_device(sizes, injections, shift_factors, line_limits, overload_cost):
    nb, nl, ns = sizes
    r, _, bx = injections.shape
    lines, buses = shift_factors.shape
    lc = lines // ns
    w = max(128, lc // 8)
    ch = w // 2
    nbuf = 8
    tw = max(128, bx // 4)
    bt = max(128, bx // 2)
    kc, nt = lc // w, bx // tw
    own_rows = nb * r
    rows = ns * own_rows
    dims = (nb, nl, ns, r, bx, lc, w, ch, nbuf, tw, bt)
    vmem, dma = pltpu.VMEM, pltpu.SemaphoreType.DMA
    whole = pl.BlockSpec(memory_space=pltpu.VMEM)
    results = pl.pallas_call(
        functools.partial(kernel, dims),
        out_shape=(
            jax.ShapeDtypeStruct((r, lines), F32),
            jax.ShapeDtypeStruct((r, nb, bx), F32),
        ),
        in_specs=[whole, whole, whole, pl.BlockSpec(memory_space=pl.ANY)],
        out_specs=(whole, whole),
        scratch_shapes=[
            vmem((nb, r, bx), F32),
            vmem((nl, rows, bx), F32),
            vmem((2 * rows, buses), BF16),
            vmem((nbuf, ch, buses), F32),
            vmem((lc, buses), BF16),
            vmem((lc, buses), BF16),
            vmem((2 * kc, rows // 2, w), F32),
            vmem((2 * kc, rows // 2, w), F32),
            vmem((2 * kc, rows // 2, w), F32),
            vmem((2 * kc, rows // 2, w), F32),
            vmem((2 * kc, rows // 2, w), F32),
            vmem((rows, w), F32),
            vmem((2 * rows, w), BF16),
            vmem((ns - 1, r, lc), F32),
            vmem((ns - 1, r, lc), F32),
            vmem((rows, buses), F32),
            vmem((ns - 1, own_rows, buses), F32),
            vmem((nl - 1, own_rows, bx), F32),
            vmem((nl - 1, own_rows, bx), F32),
            vmem((own_rows, bx), F32),
            vmem((own_rows, bx), F32),
            dma((nbuf,)),
            dma((nb,)),
            dma((nl, nb)),
            dma((nl, nb, ns)),
            dma((nl, nb, ns)),
            dma((2 * kc,)),
            dma((2 * kc,)),
            dma((2 * kc,)),
            dma((2 * kc,)),
            dma((ns - 1,)),
            dma((ns - 1,)),
            dma((ns - 1, nl * nt)),
            dma((ns - 1, nl * nt)),
            dma((nl - 1, nt)),
            dma((nl - 1, nt)),
            dma((nb - 1, nt)),
            dma((nb - 1, nt)),
        ],
        compiler_params=pltpu.CompilerParams(
            collective_id=0, has_side_effects=True, vmem_limit_bytes=60 * 1024 * 1024
        ),
        cost_estimate=pl.CostEstimate(
            flops=12 * rows * lc * buses, bytes_accessed=4 * lc * buses, transcendentals=0
        ),
    )(
        injections,
        line_limits.reshape(ns * kc, 1, w),
        overload_cost.reshape(ns * kc, 1, w),
        shift_factors,
    )
    anywhere = pl.BlockSpec(memory_space=pl.ANY)
    return pl.pallas_call(
        hand_on,
        out_shape=tuple(jax.ShapeDtypeStruct(a.shape, a.dtype) for a in results),
        in_specs=[anywhere, anywhere],
        out_specs=(anywhere, anywhere),
        scratch_shapes=[dma((2,))],
    )(*results)


def solution(mesh):
    sizes = tuple(mesh.shape[a] for a in ("bus", "line", "scen"))
    in_specs = (P(("grp", "bus", "scen"), None, "line"), P("line", "bus"), P("line"), P("line"))
    out_specs = (P(("grp", "bus", "scen"), "line"), P(("grp", "bus", "scen"), None, "line"))
    return jax.shard_map(
        functools.partial(on_device, sizes),
        mesh=mesh, in_specs=in_specs, out_specs=out_specs, check_vma=False,
    )
```

```python
import functools

import jax
import jax.numpy as jnp
from jax import lax
from jax.experimental import pallas as pl
from jax.experimental.pallas import tpu as pltpu
from jax.sharding import PartitionSpec as P

MESH = pl.DeviceIdType.MESH
F32 = jnp.float32
BF16 = jnp.bfloat16


def split(value):
    high = value.astype(BF16)
    return high, (value - high.astype(F32)).astype(BF16)


def dot_nt(a, b):
    return lax.dot_general(a, b, (((1,), (1,)), ((), ())), preferred_element_type=F32)


def dot_nn(a, b):
    return jnp.dot(a, b, preferred_element_type=F32)


def kernel(
    dims, inj, lim, cost, fac, flow_out, grad_out,
    snd, xbuf, xs, stage, fhi, flo, p, s_right, s_left, r_left, r_right,
    tot, ss, fsend, frecv, g, gc, hs, hx, own, gout,
    ld_sem, z_send, x_send, c_send, b_recv, right_send, left_send, left_recv, right_recv,
    f_send, f_recv, gc_send, gc_recv, hx_send, hx_recv, go_send, go_recv,
):
    nb, nl, ns, r, bx, lc, w, ch, nbuf, tw = dims
    z, x, c = lax.axis_index("bus"), lax.axis_index("line"), lax.axis_index("scen")
    kc, nch, nt = lc // w, lc // ch, bx // tw
    own_rows = nb * r
    rows = ns * own_rows

    def remote(src, dst, send, recv, where):
        return pltpu.make_async_remote_copy(
            src_ref=src, dst_ref=dst, send_sem=send, recv_sem=recv,
            device_id=where, device_id_type=MESH,
        )

    def load(i):
        start = pl.multiple_of(c * lc + i * ch, ch)
        slot = lax.rem(i, nbuf)
        return pltpu.make_async_copy(fac.at[pl.ds(start, ch), :], stage.at[slot], ld_sem.at[slot])

    for i in range(min(nbuf, nch)):
        load(jnp.int32(i)).start()

    barrier = pltpu.get_barrier_semaphore()
    for axis, here, count in (("bus", z, nb), ("line", x, nl), ("scen", c, ns)):
        for d in range(1, count):
            pl.semaphore_signal(
                barrier, inc=1, device_id={axis: lax.rem(here + d, count)}, device_id_type=MESH
            )

    for k in range(nb):
        snd[k] = inj[:, k, :]
    g[...] = jnp.zeros_like(g)
    pl.semaphore_wait(barrier, nb + nl + ns - 3)

    def block(xh, zz, cc):
        return xbuf.at[xh, pl.ds(pl.multiple_of((cc * nb + zz) * r, r), r), :]

    def over_bus(d):
        to = lax.rem(z + d, nb)
        return remote(snd.at[to], block(x, z, c), z_send.at[d], b_recv.at[x, z, c], {"bus": to})

    def over_line(dx, d):
        zz = lax.rem(z + nb - d, nb)
        return remote(
            block(x, zz, c), block(x, zz, c), x_send.at[dx, d], b_recv.at[x, zz, c],
            {"line": lax.rem(x + dx, nl)},
        )

    def over_core(dx, d, dc):
        zz, xh = lax.rem(z + nb - d, nb), lax.rem(x + nl - dx, nl)
        return remote(
            block(xh, zz, c), block(xh, zz, c), c_send.at[dx, d, dc], b_recv.at[xh, zz, c],
            {"scen": lax.rem(c + dc, ns)},
        )

    def arrived(xh, zz, cc):
        remote(
            block(xh, zz, cc), block(xh, zz, cc), z_send.at[0], b_recv.at[xh, zz, cc],
            {"bus": lax.rem(z + 1, nb)},
        ).wait_recv()

    for d in range(1, nb):
        over_bus(d).start()
    start_row = pl.multiple_of((c * nb + z) * r, r)
    xbuf[x, pl.ds(start_row, r), :] = snd[z]

    def forward(d):
        for dx in range(1, nl):
            over_line(dx, d).start()
        for dc in range(1, ns):
            over_core(0, d, dc).start()

    forward(0)

    def convert(i, carry):
        load(i).wait()
        slot = lax.rem(i, nbuf)
        high, low = split(stage[slot])
        at = pl.ds(pl.multiple_of(i * ch, ch), ch)
        fhi[at, :] = high
        flo[at, :] = low

        @pl.when(i + nbuf < nch)
        def _():
            load(i + nbuf).start()

        return carry

    for n in range(1, nb + 1):
        lax.fori_loop((n - 1) * nch // nb, n * nch // nb, convert, 0)
        if n < nb:
            arrived(x, lax.rem(z + nb - n, nb), c)
            forward(n)
        for dx in range(1, nl):
            xh, zz = lax.rem(x + nl - dx, nl), lax.rem(z + nb - n + 1, nb)
            arrived(xh, zz, c)
            for dc in range(1, ns):
                over_core(dx, n - 1, dc).start()

    for dc in range(1, ns):
        for dx in range(nl):
            for d in range(nb):
                arrived(lax.rem(x + nl - dx, nl), lax.rem(z + nb - d, nb), lax.rem(c + dc, ns))

    for xh in range(nl):
        high, low = split(xbuf[xh])
        xs[:rows, xh * bx:(xh + 1) * bx] = high
        xs[rows:, xh * bx:(xh + 1) * bx] = low

    def to_right(src, k):
        return remote(
            src.at[k], r_left.at[k], right_send.at[k], left_recv.at[k],
            {"bus": lax.rem(z + 1, nb)},
        )

    def to_left(src, k):
        return remote(
            src.at[k], r_right.at[k], left_send.at[k], right_recv.at[k],
            {"bus": lax.rem(z + nb - 1, nb)},
        )

    lag_left = jnp.where(z == nb - 1, kc, jnp.minimum(2 * z, kc - 1))
    lag_right = jnp.where(z == 0, kc, jnp.minimum(2 * (nb - 1 - z), kc - 1))

    def relay(s):
        k = s - lag_left

        @pl.when((z > 0) & (k >= 0) & (k < kc))
        def _():
            to_right(s_right, k).wait_recv()

            @pl.when(z < nb - 1)
            def _():
                s_right[k] = r_left[k] + p[k]
                to_right(s_right, k).start()

        m = s - lag_right

        @pl.when((z < nb - 1) & (m >= 0) & (m < kc))
        def _():
            to_left(s_left, m).wait_recv()

            @pl.when(z > 0)
            def _():
                s_left[m] = r_right[m] + p[m]
                to_left(s_left, m).start()

    def lines_of(k):
        return pl.ds(pl.multiple_of(k * w, w), w)

    def forward_chunk(k, carry):
        both = dot_nt(xs[...], fhi[lines_of(k), :])
        p[k] = both[:rows] + both[rows:] + dot_nt(xs[:rows, :], flo[lines_of(k), :])

        @pl.when(z == 0)
        def _():
            to_right(p, k).start()

        @pl.when(z == nb - 1)
        def _():
            to_left(p, k).start()

        relay(k)
        return carry

    lax.fori_loop(0, kc, forward_chunk, 0)

    def slopes(k):
        tot[...] = p[k]

        @pl.when(z > 0)
        def _():
            tot[...] += r_left[k]

        @pl.when(z < nb - 1)
        def _():
            tot[...] += r_right[k]

        at = pl.ds(pl.multiple_of(c * lc + k * w, w), w)
        flow_out[:, at] = tot[pl.ds(pl.multiple_of((c * nb + z) * r, r), r), :]
        for dc in range(1, ns):
            other = lax.rem(c + dc, ns)
            fsend[dc - 1, :, lines_of(k)] = tot[pl.ds(pl.multiple_of((other * nb + z) * r, r), r), :]
        limits = lim[c * kc + k].astype(F32) / 100.0
        t = tot[...]
        slope = 2.0 * cost[c * kc + k] * (
            jnp.maximum(t - limits, 0.0) - jnp.maximum(-t - limits, 0.0)
        )
        high, low = split(slope)
        ss[:rows, :] = high
        ss[rows:, :] = low

    def backward_tile(k, col):
        cols = pl.ds(col, tw)
        both = dot_nn(ss[...], fhi[lines_of(k), cols])
        g[:, cols] += both[:rows] + both[rows:] + dot_nn(ss[:rows, :], flo[lines_of(k), cols])

    def backward_chunk(k, carry):
        relay(kc + k)
        slopes(k)

        def tile(t, carry2):
            backward_tile(k, pl.multiple_of(t * tw, tw))
            return carry2

        lax.fori_loop(0, nl * nt, tile, 0)
        return carry

    lax.fori_loop(0, kc - 1, backward_chunk, 0)
    last = kc - 1
    relay(jnp.int32(kc + last))
    slopes(last)

    def flows_over(dc):
        return remote(
            fsend.at[dc - 1], frecv.at[dc - 1], f_send.at[dc - 1], f_recv.at[dc - 1],
            {"scen": lax.rem(c + dc, ns)},
        )

    for dc in range(1, ns):
        flows_over(dc).start()

    order = [(dx, t) for dx in range(1, nl + 1) for t in range(nt)]

    def column(dx, t):
        return pl.multiple_of(lax.rem(x + dx, nl) * bx + t * tw, tw)

    def grad_core(i, dc):
        cols = pl.ds(column(*order[i]), tw)
        other = lax.rem(c + dc, ns)
        return remote(
            g.at[pl.ds(pl.multiple_of(other * own_rows, own_rows), own_rows), cols],
            gc.at[dc - 1, :, cols], gc_send.at[dc - 1, i], gc_recv.at[dc - 1, i], {"scen": other},
        )

    def grad_line(dx, t):
        cols = pl.ds(t * tw, tw)
        return remote(
            hs.at[dx - 1, :, cols], hx.at[dx - 1, :, cols],
            hx_send.at[dx - 1, t], hx_recv.at[dx - 1, t], {"line": lax.rem(x + dx, nl)},
        )

    def grad_bus(d, t):
        cols = pl.ds(t * tw, tw)
        to = lax.rem(z + d, nb)
        return remote(
            own.at[pl.ds(pl.multiple_of(to * r, r), r), cols],
            gout.at[pl.ds(pl.multiple_of(z * r, r), r), cols],
            go_send.at[d - 1, t], go_recv.at[d - 1, t], {"bus": to},
        )

    for i, (dx, t) in enumerate(order):
        backward_tile(last, column(dx, t))
        for dc in range(1, ns):
            grad_core(i, dc).start()

    mine = pl.ds(pl.multiple_of(c * own_rows, own_rows), own_rows)
    for i, (dx, t) in enumerate(order):
        cols = pl.ds(column(dx, t), tw)
        total = g[mine, cols]
        for dc in range(1, ns):
            grad_core(i, dc).wait_recv()
            total = total + gc[dc - 1, :, cols]
        if dx < nl:
            hs[dx - 1, :, t * tw:(t + 1) * tw] = total
            grad_line(dx, t).start()
        else:
            for e in range(1, nl):
                grad_line(e, t).wait_recv()
                total = total + hx[e - 1, :, t * tw:(t + 1) * tw]
            own[:, t * tw:(t + 1) * tw] = total
            for d in range(1, nb):
                grad_bus(d, t).start()

    for dc in range(1, ns):
        flows_over(dc).wait_recv()
        sender = lax.rem(c + ns - dc, ns)
        flow_out[:, pl.ds(pl.multiple_of(sender * lc, lc), lc)] = frecv[dc - 1]

    here = pl.ds(pl.multiple_of(z * r, r), r)
    gout[here, :] = own[here, :]

    for d in range(1, nb):
        over_bus(d).wait_send()
    for d in range(nb):
        for dx in range(1, nl):
            over_line(dx, d).wait_send()
        for dx in range(nl):
            for dc in range(1, ns):
                over_core(dx, d, dc).wait_send()

    def sent(k, carry):
        @pl.when(z < nb - 1)
        def _():
            to_right(p, k).wait_send()

        @pl.when(z > 0)
        def _():
            to_left(p, k).wait_send()

        return carry

    lax.fori_loop(0, kc, sent, 0)
    for dc in range(1, ns):
        flows_over(dc).wait_send()
        for i in range(len(order)):
            grad_core(i, dc).wait_send()
    for t in range(nt):
        for dx in range(1, nl):
            grad_line(dx, t).wait_send()
        for d in range(1, nb):
            grad_bus(d, t).wait_recv()
            grad_bus(d, t).wait_send()
    for k in range(nb):
        grad_out[:, k, :] = gout[k * r:(k + 1) * r, :]


def on_device(sizes, injections, shift_factors, line_limits, overload_cost):
    nb, nl, ns = sizes
    r, _, bx = injections.shape
    lines, buses = shift_factors.shape
    lc = lines // ns
    w = max(128, lc // 8)
    ch = w // 2
    nbuf = 4
    tw = max(128, bx // 2)
    kc, nt = lc // w, bx // tw
    own_rows = nb * r
    rows = ns * own_rows
    dims = (nb, nl, ns, r, bx, lc, w, ch, nbuf, tw)
    vmem, dma = pltpu.VMEM, pltpu.SemaphoreType.DMA
    whole = pl.BlockSpec(memory_space=pltpu.VMEM)
    return pl.pallas_call(
        functools.partial(kernel, dims),
        out_shape=(
            jax.ShapeDtypeStruct((r, lines), F32),
            jax.ShapeDtypeStruct((r, nb, bx), F32),
        ),
        in_specs=[whole, whole, whole, pl.BlockSpec(memory_space=pl.ANY)],
        out_specs=(whole, whole),
        scratch_shapes=[
            vmem((nb, r, bx), F32),
            vmem((nl, rows, bx), F32),
            vmem((2 * rows, buses), BF16),
            vmem((nbuf, ch, buses), F32),
            vmem((lc, buses), BF16),
            vmem((lc, buses), BF16),
            vmem((kc, rows, w), F32),
            vmem((kc, rows, w), F32),
            vmem((kc, rows, w), F32),
            vmem((kc, rows, w), F32),
            vmem((kc, rows, w), F32),
            vmem((rows, w), F32),
            vmem((2 * rows, w), BF16),
            vmem((ns - 1, r, lc), F32),
            vmem((ns - 1, r, lc), F32),
            vmem((rows, buses), F32),
            vmem((ns - 1, own_rows, buses), F32),
            vmem((nl - 1, own_rows, bx), F32),
            vmem((nl - 1, own_rows, bx), F32),
            vmem((own_rows, bx), F32),
            vmem((own_rows, bx), F32),
            dma((nbuf,)),
            dma((nb,)),
            dma((nl, nb)),
            dma((nl, nb, ns)),
            dma((nl, nb, ns)),
            dma((kc,)),
            dma((kc,)),
            dma((kc,)),
            dma((kc,)),
            dma((ns - 1,)),
            dma((ns - 1,)),
            dma((ns - 1, nl * nt)),
            dma((ns - 1, nl * nt)),
            dma((nl - 1, nt)),
            dma((nl - 1, nt)),
            dma((nb - 1, nt)),
            dma((nb - 1, nt)),
        ],
        compiler_params=pltpu.CompilerParams(
            collective_id=0, has_side_effects=True, vmem_limit_bytes=58 * 1024 * 1024
        ),
        cost_estimate=pl.CostEstimate(
            flops=12 * rows * lc * buses, bytes_accessed=4 * lc * buses, transcendentals=0
        ),
    )(
        injections,
        line_limits.reshape(ns * kc, 1, w),
        overload_cost.reshape(ns * kc, 1, w),
        shift_factors,
    )


def solution(mesh):
    sizes = tuple(mesh.shape[a] for a in ("bus", "line", "scen"))
    in_specs = (P(("grp", "bus", "scen"), None, "line"), P("line", "bus"), P("line"), P("line"))
    out_specs = (P(("grp", "bus", "scen"), "line"), P(("grp", "bus", "scen"), None, "line"))
    return jax.shard_map(
        functools.partial(on_device, sizes),
        mesh=mesh, in_specs=in_specs, out_specs=out_specs, check_vma=False,
    )
```
